256 devices in a mesh: ctx: 8 (over x_hi, y), exp: 16 (over x_lo, z), tp: 2 (over core).
Axes of the slice: x: 4 (x_hi: 2, x_lo: 2; x = x_hi * 2 + x_lo), y: 4, z: 8, core: 2. Of those that a mesh axis runs over, the one named last changes fastest.
Arguments:
- tokens: bfloat16 [512, 6144], P(('ctx', 'exp'), 'tp'), may hold values from -6 to 6
- expert_ids: int32 [512, 4], P(('ctx', 'exp')), may hold values from 0 to 15, all different within a row; in each aligned block of 4 rows (0 to 3, 4 to 7, ...) at most 2 rows name the same one
- combine_weights: float32 [512, 4], P(('ctx', 'exp')), may hold values from 0.2 to 1
- cotangent: bfloat16 [512, 6144], P(('ctx', 'exp'), 'tp'), may hold values from -6 to 6
- gate_weight: bfloat16 [16, 6144, 8064], P('exp', None, ('ctx', 'tp')), may hold values from -0.078125 to 0.078125
- down_weight: bfloat16 [16, 8064, 6144], P('exp', ('ctx', 'tp')), may hold values from -0.0625 to 0.0625
Outputs:
- layer_out: bfloat16 [512, 6144], P(('ctx', 'exp'), 'tp')
- token_grad: bfloat16 [512, 6144], P(('ctx', 'exp'), 'tp')
- weight_grad: float32 [512, 4], P(('ctx', 'exp'))
The draws below stay inside these ranges and needn't reach their ends.
Inputs may be any that keep to these rules, and one draw needn't show every extreme that they name: `expert_ids`: within the 4 rows of one group (aligned blocks), no expert is named by more than 2 rows, and in some block one expert is named by exactly 2.
All inputs are finite; a program needn't handle non-finite values.
Results may differ from the reference program's by a relative error of at most 0.029.
Values may be sent and summed in bfloat16 or wider, within the bound.
No kernel may reach another device: no remote copies, remote signals or barrier semaphores. Data moves between devices by JAX's collectives and lax.ppermute only.
A program may use at most 128 MiB of HBM per device.

```python
import math
import jax
import jax.numpy as jnp
import numpy as np
from jax import lax

D = 6144
FFW = 8064
TOP = 4
TOK_DEV = 4
EXPERTS = 16
CAP = 2
GROUPS = 128
TOKENS = 512
N_CTX = 8
N_TP = 2


def level_of(rng, dims, shards, low, high):
    factor_of, own = 1.0, jax.random.fold_in(rng, 6)
    for axis_at, shards_of in shards:
        draws = jnp.exp(jax.random.uniform(jax.random.fold_in(own, axis_at), (shards_of,), jnp.float32, low / len(shards), high / len(shards)))
        factor_of = factor_of * jnp.repeat(draws, dims[axis_at] // shards_of).reshape([-1 if axis == axis_at else 1 for axis in range(len(dims))])
    return factor_of


def shared_out(own_key, own, number, rows, count, top, bound, skew):
    sequence = jax.random.permutation(own_key, count)
    packed, common = shares(count, rows * top, bound, skew, True), shares(count, rows * top, bound, skew, False)
    places = jnp.arange(count)

    def named(sizes, turn):
        used = int((sizes > 0).sum())
        fixed = max(1, used // 4)
        shifted = fixed + (places - fixed + turn * (used - fixed)) % max(1, count - fixed)
        return jnp.zeros((count,), jnp.int32).at[sequence[jnp.where(places < fixed, places, shifted)]].set(jnp.asarray(sizes, jnp.int32))

    sizes = jnp.where(number % 4 == 0, named(packed, number // 4), named(common, number - number // 4 - 1))
    mixed = jax.random.permutation(jax.random.fold_in(own, 3), count)
    giver, receiver = mixed[0:count // 2 * 2:2], mixed[1:count // 2 * 2:2]
    margin = jnp.minimum(sizes[giver] - 1, bound - sizes[receiver]) // 2
    margin = jnp.where((giver == sequence[0]) | (receiver == sequence[0]) | (sizes[receiver] == 0), 0, jnp.maximum(margin, 0))
    shifted = jax.random.randint(jax.random.fold_in(own, 4), (count // 2,), 0, 1 << 20) % (margin + 1)
    sizes = sizes.at[giver].add(-shifted).at[receiver].add(shifted)
    items = jnp.searchsorted(jnp.cumsum(sizes), jnp.arange(rows * top), side="right").astype(jnp.int32)
    table = items.reshape(top, rows).T
    table = table[jax.random.permutation(jax.random.fold_in(own, 1), rows)]
    turn = jax.random.randint(jax.random.fold_in(own, 2), (rows, 1), 0, top)
    return jnp.take_along_axis(table, (jnp.arange(top)[None, :] + turn) % top, axis=1)


def shares(count, total, bound, skew, full):
    portions = [(1 << 20) // math.isqrt(grade ** skew) + 1 for grade in range(1, count + 1)]
    largest = bound if full else min(bound, max(-(-total // count), total * portions[0] // sum(portions)))
    least = 1 if total - largest >= count - 1 else 0
    given, rest = [largest] + [least] * (count - 1), total - largest - least * (count - 1)
    while rest > 0:
        candidates = [i for i in range(1, count) if given[i] < largest] or [i for i in range(1, count) if given[i] < bound]
        pool, budget = sum([portions[i] for i in candidates]), rest
        for i in candidates:
            extra = min(bound - given[i], max(1, budget * portions[i] // pool), rest)
            given[i] = given[i] + extra
            rest = rest - extra
    return np.array(given)


def normal_values(stream_key, shape, deviation, limit, pieces=(), kind=jnp.bfloat16):
    array = jax.random.normal(stream_key, shape, jnp.float32) * deviation
    if len(pieces) > 0:
        array = level_of(stream_key, shape, pieces, -0.22, 0.18) * array
    return jnp.clip(array, min=-limit, max=limit).astype(kind)


def setup_inputs(seed: int = 0) -> dict:
    key_of = jax.random.split(jax.random.key(seed), 7)
    tokens = normal_values(key_of[0], (TOKENS, D), 1.0, 6.0, ((0, 128), (1, 2)))
    expert_ids_keys = jax.random.split(jax.random.fold_in(key_of[1], 1), TOKENS // TOK_DEV)
    expert_ids_turns = jax.random.permutation(jax.random.fold_in(key_of[1], 3), TOKENS // TOK_DEV)
    expert_ids = jax.vmap(lambda own, number: shared_out(jax.random.fold_in(key_of[1], 2), own, number, TOK_DEV, EXPERTS, TOP, CAP, 2))(expert_ids_keys, expert_ids_turns).reshape((TOKENS, TOP))
    combine_weights = jnp.clip(0.2 + 0.8 * jax.random.uniform(key_of[2], (TOKENS, TOP), jnp.float32) ** level_of(key_of[2], (TOKENS, TOP), ((0, 128),), -0.2, 0.2), 0.2, 1.0)
    cotangent = normal_values(key_of[3], (TOKENS, D), 1.0, 6.0, ((0, 128), (1, 2)))
    gate_weight = normal_values(key_of[4], (EXPERTS, D, FFW), D ** -0.5, 0.078125, ((0, 16), (2, 16)))
    down_weight = normal_values(key_of[5], (EXPERTS, FFW, D), FFW ** -0.5, 0.0625, ((0, 16), (1, 16)))
    return dict(tokens=tokens, expert_ids=expert_ids, combine_weights=combine_weights, cotangent=cotangent, gate_weight=gate_weight, down_weight=down_weight)


def silu_slope(value):
    sigma = jax.nn.sigmoid(value)
    return sigma * (1.0 + value * (1.0 - sigma))


def blocked_sum(left, right):
    blocks = N_CTX * N_TP
    piece_width = FFW // blocks
    lhs = left.reshape(left.shape[0], blocks, piece_width).astype(jnp.float32)
    rhs = right.reshape(blocks, piece_width, right.shape[1]).astype(jnp.float32)
    parts = jnp.einsum('rbf,bfd->brd', lhs, rhs, precision=lax.Precision.HIGHEST)
    rounded = lax.optimization_barrier(parts.astype(jnp.bfloat16))
    return jnp.sum(rounded.astype(jnp.float32), 0).astype(jnp.bfloat16)


def expert_pass(operands):
    rows, grads, gate_w, down_w = operands
    gate_pre = jnp.dot(rows, gate_w, preferred_element_type=jnp.float32)
    hidden = jax.nn.silu(gate_pre).astype(jnp.bfloat16)
    out_rows = blocked_sum(hidden, down_w)
    hidden_grad = jnp.dot(grads, down_w.T, preferred_element_type=jnp.float32)
    pre_grad = (hidden_grad * silu_slope(gate_pre)).astype(jnp.bfloat16)
    back_rows = blocked_sum(pre_grad, gate_w.T)
    return out_rows, back_rows


def reference(tokens, expert_ids, combine_weights, cotangent, gate_weight, down_weight):
    highest = lax.Precision.HIGHEST
    pair_count = TOK_DEV * TOP
    flattened = expert_ids.reshape(GROUPS, pair_count)
    onehot = (flattened[:, :, None] == jnp.arange(EXPERTS, dtype=jnp.int32)[None, None, :]).astype(jnp.int32)
    before = jnp.cumsum(onehot, 1) - onehot
    slot_index = jnp.sum(onehot * before, 2)
    position = flattened * CAP + slot_index
    placing = (jnp.arange(EXPERTS * CAP, dtype=jnp.int32)[None, :, None] == position[:, None, :]).astype(jnp.float32)
    per_token = placing.reshape(GROUPS, EXPERTS * CAP, TOK_DEV, TOP)
    chosen = jnp.sum(per_token, 3)
    weighted = jnp.sum(per_token * combine_weights.reshape(GROUPS, 1, TOK_DEV, TOP), 3)
    token_rows = tokens.reshape(GROUPS, TOK_DEV, D).astype(jnp.float32)
    cot_rows = cotangent.reshape(GROUPS, TOK_DEV, D).astype(jnp.float32)
    dispatched = jnp.einsum('gjn,gnd->gjd', chosen, token_rows, precision=highest).astype(jnp.bfloat16)
    dispatched_grad = jnp.einsum('gjn,gnd->gjd', weighted, cot_rows, precision=highest).astype(jnp.bfloat16)

    def by_expert(table):
        return table.reshape(GROUPS, EXPERTS, CAP, D).transpose(1, 0, 2, 3).reshape(EXPERTS, GROUPS * CAP, D)

    def by_group(table):
        return table.reshape(EXPERTS, GROUPS, CAP, D).transpose(1, 0, 2, 3).reshape(GROUPS, EXPERTS * CAP, D).astype(jnp.float32)

    out_rows, back_rows = lax.map(expert_pass, (by_expert(dispatched), by_expert(dispatched_grad), gate_weight, down_weight))
    out_group = by_group(out_rows)
    back_group = by_group(back_rows)
    layer_out = jnp.einsum('gjn,gjd->gnd', weighted, out_group, precision=highest).reshape(TOKENS, D).astype(jnp.bfloat16)
    token_grad = jnp.einsum('gjn,gjd->gnd', chosen, back_group, precision=highest).reshape(TOKENS, D).astype(jnp.bfloat16)
    picked = jnp.einsum('gjl,gjd->gld', placing, out_group, precision=highest).reshape(GROUPS, TOK_DEV, TOP, D)
    weight_grad = jnp.sum(picked * cot_rows[:, :, None, :], 3).reshape(TOKENS, TOP)
    return layer_out, token_grad, weight_grad
```

```python
import jax
import jax.numpy as jnp
from jax import lax
from jax.sharding import PartitionSpec as P

AXES = ("ctx", "exp", "tp")
ROW_SPLIT = 2


def shift_pairs(sizes, hi=0, row=0, core=0):
    contexts, experts, cores = sizes
    rows = contexts // ROW_SPLIT
    pairs = []
    for c in range(contexts):
        h, y = divmod(c, rows)
        target = (h + hi) % ROW_SPLIT * rows + (y + row) % rows
        for e in range(experts):
            for t in range(cores):
                pairs.append(
                    ((c * experts + e) * cores + t, (target * experts + e) * cores + (t + core) % cores)
                )
    return pairs


def shards(sizes, tokens, expert_ids, combine_weights, cotangent, gate_weight, down_weight):
    tok_count, half_width = tokens.shape
    top_count = expert_ids.shape[1]
    gate = gate_weight[0]
    down = down_weight[0]
    experts = sizes[1]
    capacity = 2
    member_rows = experts * capacity
    highest = lax.Precision.HIGHEST
    core = lax.axis_index("tp")

    def move(value, **shift):
        return lax.ppermute(value, AXES, shift_pairs(sizes, **shift))

    flattened = expert_ids.reshape(-1)
    onehot = (flattened[:, None] == jnp.arange(experts, dtype=jnp.int32)[None, :]).astype(jnp.int32)
    before = jnp.cumsum(onehot, 0) - onehot
    slot_index = jnp.sum(onehot * before, 1)
    position = flattened * capacity + slot_index
    placing = (
        jnp.arange(member_rows, dtype=jnp.int32)[:, None] == position[None, :]
    ).astype(jnp.float32)
    per_token = placing.reshape(member_rows, tok_count, top_count)
    chosen = jnp.sum(per_token, 2)
    weighted = jnp.sum(per_token * combine_weights[None, :, :], 2)

    def exchange(rows):
        sent = rows.reshape(experts, capacity, half_width)
        got = lax.all_to_all(sent, "exp", split_axis=0, concat_axis=0, tiled=True)
        return got.reshape(member_rows, half_width)

    def gather(block):
        across = move(block, hi=1)
        below = move(block, row=1)
        above = move(block, row=-1)
        far = move(block, row=2)
        across_below = move(across, row=1)
        across_above = move(across, row=-1)
        across_far = move(far, hi=1)
        mine = jnp.concatenate(
            [block, across, below, above, far, across_below, across_above, across_far], 0
        )
        other = move(mine, core=1)
        first = jnp.where(core == 0, mine, other)
        second = jnp.where(core == 0, other, mine)
        return jnp.concatenate([first, second], 1)

    def scatter(partial):
        kept = lax.dynamic_slice_in_dim(partial, core * half_width, half_width, 1)
        given = lax.dynamic_slice_in_dim(partial, (1 - core) * half_width, half_width, 1)
        got = move(given, core=1)
        total = (kept.astype(jnp.float32) + got.astype(jnp.float32)).astype(jnp.bfloat16)
        own, across, below, above, far, across_below, across_above, across_far = [
            total[i * member_rows : (i + 1) * member_rows] for i in range(8)
        ]

        def add(*terms):
            return sum(t.astype(jnp.float32) for t in terms).astype(jnp.bfloat16)

        from_above = move(across_below, row=-1)
        from_below = move(across_above, row=1)
        from_across = move(across_far, hi=1)
        direct_above = move(below, row=-1)
        direct_below = move(above, row=1)
        turned = move(add(across, from_above, from_below), hi=1)
        direct_far = move(add(far, from_across), row=2)
        return add(own, direct_above, direct_below, turned, direct_far)

    dispatched = jnp.dot(
        chosen.astype(jnp.bfloat16), tokens, preferred_element_type=jnp.float32
    ).astype(jnp.bfloat16)
    dispatched_grad = jnp.dot(weighted, cotangent.astype(jnp.float32), precision=highest).astype(
        jnp.bfloat16
    )
    token_block = exchange(dispatched)
    grad_block = exchange(dispatched_grad)
    routed_rows = gather(token_block)
    routed_grad = gather(grad_block)
    gate_pre = jnp.dot(routed_rows, gate, preferred_element_type=jnp.float32)
    sigma = jax.nn.sigmoid(gate_pre)
    hidden = (gate_pre * sigma).astype(jnp.bfloat16)
    out_partial = jnp.dot(hidden, down, preferred_element_type=jnp.float32).astype(jnp.bfloat16)
    hidden_grad = lax.dot_general(
        routed_grad, down, (((1,), (1,)), ((), ())), preferred_element_type=jnp.float32
    )
    pre_grad = (hidden_grad * sigma * (1.0 + gate_pre * (1.0 - sigma))).astype(jnp.bfloat16)
    back_partial = lax.dot_general(
        pre_grad, gate, (((1,), (1,)), ((), ())), preferred_element_type=jnp.float32
    ).astype(jnp.bfloat16)
    out_rows = exchange(scatter(out_partial))
    back_rows = exchange(scatter(back_partial))

    out_sum = jnp.dot(weighted.T, out_rows.astype(jnp.float32), precision=highest)
    back_sum = jnp.dot(chosen.T.astype(jnp.bfloat16), back_rows, preferred_element_type=jnp.float32)
    products = lax.dot_general(
        cotangent, out_rows, (((1,), (1,)), ((), ())), preferred_element_type=jnp.float32
    )
    partial_pairs = jnp.einsum("nj,jnk->nk", products, per_token, precision=highest)
    weight_grad = lax.psum(partial_pairs, "tp")
    return (out_sum.astype(jnp.bfloat16), back_sum.astype(jnp.bfloat16), weight_grad)


def solution(mesh):
    sizes = tuple(mesh.shape[name] for name in AXES)

    def block(*args):
        return shards(sizes, *args)

    in_specs = (
        P(("ctx", "exp"), "tp"),
        P(("ctx", "exp"), None),
        P(("ctx", "exp"), None),
        P(("ctx", "exp"), "tp"),
        P("exp", None, ("ctx", "tp")),
        P("exp", ("ctx", "tp"), None),
    )
    out_specs = (P(("ctx", "exp"), "tp"), P(("ctx", "exp"), "tp"), P(("ctx", "exp"), None))
    return jax.shard_map(block, mesh=mesh, in_specs=in_specs, out_specs=out_specs, check_vma=False)
```

```python
import functools

import jax
import jax.numpy as jnp
from jax import lax
from jax.experimental import pallas as pl
from jax.experimental.pallas import tpu as pltpu
from jax.sharding import PartitionSpec as P

AXES = ("ctx", "exp", "tp")
ROW_SPLIT = 2


def shift_pairs(sizes, hi=0, row=0, core=0):
    contexts, experts, cores = sizes
    rows = contexts // ROW_SPLIT
    pairs = []
    for c in range(contexts):
        h, y = divmod(c, rows)
        target = (h + hi) % ROW_SPLIT * rows + (y + row) % rows
        for e in range(experts):
            for t in range(cores):
                pairs.append(
                    ((c * experts + e) * cores + t, (target * experts + e) * cores + (t + core) % cores)
                )
    return pairs


NT = (((1,), (1,)), ((), ()))
TILE = 512
WHOLE = pl.BlockSpec(memory_space=pltpu.VMEM)


def half_columns(core, width, start, size):
    return pl.ds(pl.multiple_of(core * width + start, TILE), size)


def wide_product(core, mine_ref, other_ref, weight_ref):
    width = mine_ref.shape[1]
    left = lax.dot_general(
        mine_ref[...],
        weight_ref[:, half_columns(core, width, 0, width)],
        NT,
        preferred_element_type=jnp.float32,
    )
    right = lax.dot_general(
        other_ref[...],
        weight_ref[:, half_columns(1 - core, width, 0, width)],
        NT,
        preferred_element_type=jnp.float32,
    )
    return left + right


def deep_product(core, left, weight_ref, kept_ref, given_ref):
    width = kept_ref.shape[1]
    for side, out_ref in ((1 - core, given_ref), (core, kept_ref)):
        for start in range(0, width, TILE):
            out_ref[:, start : start + TILE] = jnp.dot(
                left,
                weight_ref[:, half_columns(side, width, start, TILE)],
                preferred_element_type=jnp.float32,
            ).astype(jnp.bfloat16)


def forward_kernel(core_ref, mine_ref, other_ref, gate_ref, down_ref, pre_ref, kept_ref, given_ref):
    core = core_ref[0]
    pre = wide_product(core, mine_ref, other_ref, gate_ref)
    pre_ref[...] = pre
    hidden = (pre / (1.0 + jnp.exp(-pre))).astype(jnp.bfloat16)
    deep_product(core, hidden, down_ref, kept_ref, given_ref)


def backward_kernel(core_ref, mine_ref, other_ref, down_ref, gate_ref, pre_ref, kept_ref, given_ref):
    core = core_ref[0]
    grad = wide_product(core, mine_ref, other_ref, down_ref)
    pre = pre_ref[...]
    sigma = 1.0 / (1.0 + jnp.exp(-pre))
    pre_grad = (grad * (sigma * (1.0 + pre * (1.0 - sigma)))).astype(jnp.bfloat16)
    deep_product(core, pre_grad, gate_ref, kept_ref, given_ref)


def expert_call(kernel, core, mine, other, first, second, pre=None):
    rows, width = mine.shape
    units = first.shape[0]
    half = jax.ShapeDtypeStruct((rows, width), jnp.bfloat16)
    outs = [half, half]
    args = [core, mine, other, first, second]
    if pre is None:
        outs = [jax.ShapeDtypeStruct((rows, units), jnp.float32)] + outs
    else:
        args = args + [pre]
    return pl.pallas_call(
        kernel,
        out_shape=tuple(outs),
        in_specs=[pl.BlockSpec(memory_space=pltpu.SMEM)] + [WHOLE] * (len(args) - 1),
        out_specs=tuple([WHOLE] * len(outs)),
        compiler_params=pltpu.CompilerParams(vmem_limit_bytes=24 * 1024 * 1024),
        cost_estimate=pl.CostEstimate(
            flops=8 * rows * width * units, bytes_accessed=8 * units * width, transcendentals=rows * units
        ),
    )(*args)


def load_kernel(source, target, sem):
    copy = pltpu.make_async_copy(source, target, sem)
    copy.start()
    copy.wait()


def load_weights(*weights):
    return [
        pl.pallas_call(
            load_kernel,
            out_shape=jax.ShapeDtypeStruct(weight.shape, weight.dtype),
            in_specs=[pl.BlockSpec(memory_space=pl.ANY)],
            out_specs=WHOLE,
            scratch_shapes=[pltpu.SemaphoreType.DMA],
            compiler_params=pltpu.CompilerParams(vmem_limit_bytes=44 * 1024 * 1024),
        )(weight)
        for weight in weights
    ]


def slot_positions(ids_ref, tok_count, top_count, capacity):
    names = [ids_ref[n, k] for n in range(tok_count) for k in range(top_count)]
    positions = []
    for i, name in enumerate(names):
        slot = jnp.int32(0)
        for other in names[:i]:
            slot = slot + jnp.where(other == name, 1, 0)
        positions.append(name * capacity + slot)
    return positions


def dispatch_kernel(
    capacity, core_ref, ids_ref, weights_ref, tokens_ref, cotangent_ref, sent_ref, core_out
):
    core_out[0] = core_ref[0]
    tok_count, width = tokens_ref.shape
    top_count = ids_ref.shape[1]
    rows = sent_ref.shape[0]
    positions = slot_positions(ids_ref, tok_count, top_count, capacity)
    place = lax.broadcasted_iota(jnp.int32, (rows, 1), 0)
    chosen, weighted = [], []
    for n in range(tok_count):
        plain = jnp.zeros((rows, 1), jnp.float32)
        scaled = jnp.zeros((rows, 1), jnp.float32)
        for k in range(top_count):
            here = place == positions[n * top_count + k]
            plain = jnp.where(here, 1.0, plain)
            scaled = jnp.where(here, weights_ref[n, k], scaled)
        chosen.append(plain)
        weighted.append(scaled)
    for source_ref, masks, base in ((tokens_ref, chosen, 0), (cotangent_ref, weighted, width)):
        for start in range(0, width, 512):
            values = source_ref[:, start : start + 512].astype(jnp.float32)
            total = masks[0] * values[0:1]
            for n in range(1, tok_count):
                total = total + masks[n] * values[n : n + 1]
            sent_ref[:, base + start : base + start + 512] = total.astype(jnp.bfloat16)


def dispatch_rows(core, tokens, expert_ids, combine_weights, cotangent, experts, capacity):
    scalars = pl.BlockSpec(memory_space=pltpu.SMEM)
    return pl.pallas_call(
        functools.partial(dispatch_kernel, capacity),
        out_shape=(
            jax.ShapeDtypeStruct((experts * capacity, 2 * tokens.shape[1]), jnp.bfloat16),
            jax.ShapeDtypeStruct((1,), jnp.int32),
        ),
        in_specs=[scalars, scalars, scalars, WHOLE, WHOLE],
        out_specs=(WHOLE, scalars),
        compiler_params=pltpu.CompilerParams(vmem_limit_bytes=58 * 1024 * 1024),
    )(core.reshape(1), expert_ids, combine_weights, tokens, cotangent)


def combine_kernel(capacity, ids_ref, weights_ref, returned_ref, out_ref, back_ref, pairs_ref):
    tok_count, width = out_ref.shape
    top_count = ids_ref.shape[1]
    rows = returned_ref.shape[0]
    positions = slot_positions(ids_ref, tok_count, top_count, capacity)
    line = lax.broadcasted_iota(jnp.int32, (8, rows), 0)
    place = lax.broadcasted_iota(jnp.int32, (8, rows), 1)
    chosen = jnp.zeros((8, rows), jnp.float32)
    weighted = jnp.zeros((8, rows), jnp.float32)
    lane = lax.broadcasted_iota(jnp.int32, (1, 128), 1)
    pair_place = jnp.full((1, 128), -1, jnp.int32)
    pair_weight = jnp.ones((1, 128), jnp.float32)
    for i, position in enumerate(positions):
        n, k = divmod(i, top_count)
        here = (line == n) & (place == position)
        chosen = jnp.where(here, 1.0, chosen)
        weighted = jnp.where(here, weights_ref[n, k], weighted)
        pair_place = jnp.where(lane == i, position, pair_place)
        pair_weight = jnp.where(lane == i, weights_ref[n, k], pair_weight)
    high = weighted.astype(jnp.bfloat16)
    rest = weighted - high.astype(jnp.float32)
    middle = rest.astype(jnp.bfloat16)
    low = (rest - middle.astype(jnp.float32)).astype(jnp.bfloat16)
    plain = chosen.astype(jnp.bfloat16)
    for start in range(0, width, 512):
        values = returned_ref[:, start : start + 512]
        total = jnp.dot(high, values, preferred_element_type=jnp.float32)
        total = total + jnp.dot(middle, values, preferred_element_type=jnp.float32)
        total = total + jnp.dot(low, values, preferred_element_type=jnp.float32)
        out_ref[:, start : start + 512] = total[:tok_count].astype(jnp.bfloat16)
        values = returned_ref[:, width + start : width + start + 512]
        total = jnp.dot(plain, values, preferred_element_type=jnp.float32)
        back_ref[:, start : start + 512] = total[:tok_count].astype(jnp.bfloat16)
    extra = returned_ref[:, 2 * width : 2 * width + 128].astype(jnp.float32)
    row_values = jnp.sum(extra, 1, keepdims=True)
    match = lax.broadcasted_iota(jnp.int32, (rows, 128), 0) == pair_place
    pairs = jnp.sum(jnp.where(match, row_values, 0.0), 0, keepdims=True) / pair_weight
    for n in range(tok_count):
        pairs_ref[n : n + 1, :] = pairs[:, n * top_count : (n + 1) * top_count]


def combine_rows(expert_ids, combine_weights, returned, width, capacity):
    scalars = pl.BlockSpec(memory_space=pltpu.SMEM)
    tok_count = expert_ids.shape[0]
    half = jax.ShapeDtypeStruct((tok_count, width), jnp.bfloat16)
    return pl.pallas_call(
        functools.partial(combine_kernel, capacity),
        out_shape=(half, half, jax.ShapeDtypeStruct(expert_ids.shape, jnp.float32)),
        in_specs=[scalars, scalars, WHOLE],
        out_specs=(WHOLE, WHOLE, WHOLE),
        compiler_params=pltpu.CompilerParams(vmem_limit_bytes=8 * 1024 * 1024),
    )(expert_ids, combine_weights, returned)


def shards(sizes, tokens, expert_ids, combine_weights, cotangent, gate_weight, down_weight):
    half_width = tokens.shape[1]
    gate = gate_weight[0].T
    down = down_weight[0]
    experts = sizes[1]
    capacity = 2
    member_rows = experts * capacity

    def move(value, **shift):
        return lax.ppermute(value, AXES, shift_pairs(sizes, **shift))

    def exchange(rows):
        sent = rows.reshape(experts, capacity, rows.shape[1])
        got = lax.all_to_all(sent, "exp", split_axis=0, concat_axis=0, tiled=True)
        return got.reshape(rows.shape)

    def add(*terms):
        return sum(t.astype(jnp.float32) for t in terms).astype(jnp.bfloat16)

    def gather(blocks, weights):
        stacked = jnp.concatenate(blocks, 0)
        across, far, gate, down = lax.optimization_barrier(
            (move(stacked, hi=1), move(stacked, row=2), *weights)
        )
        results = []
        for i, block in enumerate(blocks):
            part = slice(i * member_rows, (i + 1) * member_rows)
            pair = jnp.concatenate([block, across[part]], 0)
            results.append([pair, move(pair, row=1), move(pair, row=-1), far[part]])
        across_far = move(far, hi=1)
        for i, pieces in enumerate(results):
            part = slice(i * member_rows, (i + 1) * member_rows)
            mine = jnp.concatenate(pieces + [across_far[part]], 0)
            results[i] = (mine, move(mine, core=1))
        return results, gate, down

    def scatter(kept, given):
        total = add(kept, move(given, core=1))
        own, across, below, above, far, across_far = jnp.split(
            total, [member_rows * i for i in (1, 2, 4, 6, 7)], 0
        )
        got_below = move(below, row=-1)
        got_above = move(above, row=1)
        far = add(far, move(across_far, hi=1))
        across = add(across, got_below[member_rows:], got_above[member_rows:])
        got_across = move(across, hi=1)
        got_far = move(far, row=2)
        return add(own, got_below[:member_rows], got_above[:member_rows], got_across, got_far)

    sent, core = dispatch_rows(
        lax.axis_index("tp"), tokens, expert_ids, combine_weights, cotangent, experts, capacity
    )
    arrived = exchange(sent)
    arrived, gate, down = lax.optimization_barrier((arrived, gate, down))
    gate, down = load_weights(gate, down)
    grad_block = arrived[:, half_width:]
    (routed_rows, routed_grad), gate, down = gather(
        (arrived[:, :half_width], grad_block), (gate, down)
    )
    pre, out_kept, out_given = expert_call(forward_kernel, core, *routed_rows, gate, down)
    back_kept, back_given = expert_call(backward_kernel, core, *routed_grad, down, gate, pre)
    out_block = scatter(out_kept, out_given)
    pair_half = jnp.sum(
        out_block.astype(jnp.float32) * grad_block.astype(jnp.float32), 1, keepdims=True
    )
    pair_value = pair_half + move(pair_half, core=1)
    pieces = []
    for _ in range(3):
        piece = pair_value.astype(jnp.bfloat16)
        pieces.append(piece)
        pair_value = pair_value - piece.astype(jnp.float32)
    back_block = scatter(back_kept, back_given)
    extra = jnp.concatenate(pieces + [jnp.zeros((member_rows, 125), jnp.bfloat16)], 1)
    returned = exchange(jnp.concatenate([out_block, back_block, extra], 1))

    return combine_rows(expert_ids, combine_weights, returned, half_width, capacity)


def solution(mesh):
    sizes = tuple(mesh.shape[name] for name in AXES)

    def block(*args):
        return shards(sizes, *args)

    in_specs = (
        P(("ctx", "exp"), "tp"),
        P(("ctx", "exp"), None),
        P(("ctx", "exp"), None),
        P(("ctx", "exp"), "tp"),
        P("exp", None, ("ctx", "tp")),
        P("exp", ("ctx", "tp"), None),
    )
    out_specs = (P(("ctx", "exp"), "tp"), P(("ctx", "exp"), "tp"), P(("ctx", "exp"), None))
    return jax.shard_map(block, mesh=mesh, in_specs=in_specs, out_specs=out_specs, check_vma=False)
```

```python
import functools

import jax
import jax.numpy as jnp
from jax import lax
from jax.experimental import pallas as pl
from jax.experimental.pallas import tpu as pltpu
from jax.sharding import PartitionSpec as P

AXES = ("ctx", "exp", "tp")
ROW_SPLIT = 2


def shift_pairs(sizes, hi=0, row=0, core=0):
    contexts, experts, cores = sizes
    rows = contexts // ROW_SPLIT
    pairs = []
    for c in range(contexts):
        h, y = divmod(c, rows)
        target = (h + hi) % ROW_SPLIT * rows + (y + row) % rows
        for e in range(experts):
            for t in range(cores):
                pairs.append(
                    ((c * experts + e) * cores + t, (target * experts + e) * cores + (t + core) % cores)
                )
    return pairs


NT = (((1,), (1,)), ((), ()))
TILE = 512
WHOLE = pl.BlockSpec(memory_space=pltpu.VMEM)


def half_columns(core, width, start, size):
    return pl.ds(pl.multiple_of(core * width + start, TILE), size)


def wide_product(core, rows_ref, weight_ref):
    width = rows_ref.shape[1]
    return lax.dot_general(
        rows_ref[...],
        weight_ref[:, half_columns(core, width, 0, width)],
        NT,
        preferred_element_type=jnp.float32,
    )


def deep_product(core, left, weight_ref, kept_ref, given_ref):
    width = kept_ref.shape[1]
    for side, out_ref in ((1 - core, given_ref), (core, kept_ref)):
        for start in range(0, width, TILE):
            out_ref[:, start : start + TILE] = jnp.dot(
                left,
                weight_ref[:, half_columns(side, width, start, TILE)],
                preferred_element_type=jnp.float32,
            ).astype(jnp.bfloat16)


def first_kernel(core_ref, rows_ref, grads_ref, gate_ref, down_ref, pre_ref, grad_ref):
    pre_ref[...] = wide_product(core_ref[0], rows_ref, gate_ref)
    grad_ref[...] = wide_product(core_ref[0], grads_ref, down_ref)


def forward_kernel(
    core_ref, partial_ref, other_ref, gate_ref, down_ref, pre_ref, kept_ref, given_ref
):
    core = core_ref[0]
    pre = partial_ref[...] + wide_product(1 - core, other_ref, gate_ref)
    pre_ref[...] = pre
    hidden = (pre / (1.0 + jnp.exp(-pre))).astype(jnp.bfloat16)
    deep_product(core, hidden, down_ref, kept_ref, given_ref)


def backward_kernel(
    core_ref, partial_ref, other_ref, down_ref, gate_ref, pre_ref, kept_ref, given_ref
):
    core = core_ref[0]
    grad = partial_ref[...] + wide_product(1 - core, other_ref, down_ref)
    pre = pre_ref[...]
    sigma = 1.0 / (1.0 + jnp.exp(-pre))
    pre_grad = (grad * (sigma * (1.0 + pre * (1.0 - sigma)))).astype(jnp.bfloat16)
    deep_product(core, pre_grad, gate_ref, kept_ref, given_ref)


def expert_call(kernel, outs, args, products):
    rows, width = args[2].shape
    units = args[3].shape[0]
    shapes = {
        "units": jax.ShapeDtypeStruct((rows, units), jnp.float32),
        "half": jax.ShapeDtypeStruct((rows, width), jnp.bfloat16),
    }
    return pl.pallas_call(
        kernel,
        out_shape=tuple(shapes[name] for name in outs),
        in_specs=[pl.BlockSpec(memory_space=pltpu.SMEM)] + [WHOLE] * (len(args) - 1),
        out_specs=tuple([WHOLE] * len(outs)),
        compiler_params=pltpu.CompilerParams(vmem_limit_bytes=24 * 1024 * 1024),
        cost_estimate=pl.CostEstimate(
            flops=2 * products * rows * width * units,
            bytes_accessed=products * units * width,
            transcendentals=0,
        ),
    )(*args)


def load_kernel(source, target, sem):
    copy = pltpu.make_async_copy(source, target, sem)
    copy.start()
    copy.wait()


def load_weights(*weights):
    return [
        pl.pallas_call(
            load_kernel,
            out_shape=jax.ShapeDtypeStruct(weight.shape, weight.dtype),
            in_specs=[pl.BlockSpec(memory_space=pl.ANY)],
            out_specs=WHOLE,
            scratch_shapes=[pltpu.SemaphoreType.DMA],
            compiler_params=pltpu.CompilerParams(vmem_limit_bytes=44 * 1024 * 1024),
        )(weight)
        for weight in weights
    ]


def total_kernel(kept_ref, got_ref, *out_refs):
    at = 0
    for out_ref in out_refs:
        size = out_ref.shape[0]
        kept = kept_ref[at : at + size, :].astype(jnp.float32)
        out_ref[...] = (kept + got_ref[at : at + size, :].astype(jnp.float32)).astype(jnp.bfloat16)
        at = at + size


def total_blocks(kept, got, sizes):
    width = kept.shape[1]
    return pl.pallas_call(
        total_kernel,
        out_shape=tuple(jax.ShapeDtypeStruct((size, width), jnp.bfloat16) for size in sizes),
        in_specs=[WHOLE, WHOLE],
        out_specs=tuple([WHOLE] * len(sizes)),
        compiler_params=pltpu.CompilerParams(vmem_limit_bytes=12 * 1024 * 1024),
        cost_estimate=pl.CostEstimate(
            flops=kept.size, bytes_accessed=1 << 20, transcendentals=0
        ),
    )(kept, got)


def payload_kernel(out_ref, own, below, above, across, straight, pair_ref, moved_ref, sent_ref):
    rows, width = out_ref.shape
    for start in range(0, width, TILE):
        cols = slice(start, start + TILE)
        sent_ref[:, cols] = out_ref[:, cols]
        total = own[:, cols].astype(jnp.float32)
        for ref in (below, above, across, straight):
            total = total + ref[:rows, cols].astype(jnp.float32)
        sent_ref[:, width + start : width + start + TILE] = total.astype(jnp.bfloat16)
    value = pair_ref[...] + moved_ref[...]
    lane = lax.broadcasted_iota(jnp.int32, (rows, 128), 1)
    extra = jnp.zeros((rows, 128), jnp.float32)
    for i in range(3):
        piece = value.astype(jnp.bfloat16).astype(jnp.float32)
        extra = jnp.where(lane == i, piece, extra)
        value = value - piece
    sent_ref[:, 2 * width :] = extra.astype(jnp.bfloat16)


def return_payload(out_block, back_parts, pair_half, moved):
    rows, width = out_block.shape
    return pl.pallas_call(
        payload_kernel,
        out_shape=jax.ShapeDtypeStruct((rows, 2 * width + 128), jnp.bfloat16),
        in_specs=[WHOLE] * 8,
        out_specs=WHOLE,
        compiler_params=pltpu.CompilerParams(vmem_limit_bytes=8 * 1024 * 1024),
    )(out_block, *back_parts, pair_half, moved)


def slot_positions(ids_ref, tok_count, top_count, capacity):
    names = [ids_ref[n, k] for n in range(tok_count) for k in range(top_count)]
    positions = []
    for i, name in enumerate(names):
        slot = jnp.int32(0)
        for other in names[:i]:
            slot = slot + jnp.where(other == name, 1, 0)
        positions.append(name * capacity + slot)
    return positions


def dispatch_kernel(
    capacity, core_ref, ids_ref, weights_ref, tokens_ref, cotangent_ref, sent_ref, core_out
):
    core_out[0] = core_ref[0]
    tok_count, width = tokens_ref.shape
    top_count = ids_ref.shape[1]
    rows = sent_ref.shape[0] * sent_ref.shape[1]
    positions = slot_positions(ids_ref, tok_count, top_count, capacity)
    place = lax.broadcasted_iota(jnp.int32, (rows, 1), 0)
    chosen, weighted = [], []
    for n in range(tok_count):
        plain = jnp.zeros((rows, 1), jnp.float32)
        scaled = jnp.zeros((rows, 1), jnp.float32)
        for k in range(top_count):
            here = place == positions[n * top_count + k]
            plain = jnp.where(here, 1.0, plain)
            scaled = jnp.where(here, weights_ref[n, k], scaled)
        chosen.append(plain)
        weighted.append(scaled)
    for source_ref, masks, base in ((tokens_ref, chosen, 0), (cotangent_ref, weighted, width)):
        for start in range(0, width, 512):
            values = source_ref[:, start : start + 512].astype(jnp.float32)
            total = masks[0] * values[0:1]
            for n in range(1, tok_count):
                total = total + masks[n] * values[n : n + 1]
            shaped = total.astype(jnp.bfloat16).reshape(rows // capacity, capacity, 512)
            sent_ref[:, :, base + start : base + start + 512] = shaped


def dispatch_rows(core, tokens, expert_ids, combine_weights, cotangent, experts, capacity):
    scalars = pl.BlockSpec(memory_space=pltpu.SMEM)
    return pl.pallas_call(
        functools.partial(dispatch_kernel, capacity),
        out_shape=(
            jax.ShapeDtypeStruct((experts, capacity, 2 * tokens.shape[1]), jnp.bfloat16),
            jax.ShapeDtypeStruct((1,), jnp.int32),
        ),
        in_specs=[scalars, scalars, scalars, WHOLE, WHOLE],
        out_specs=(WHOLE, scalars),
        compiler_params=pltpu.CompilerParams(vmem_limit_bytes=58 * 1024 * 1024),
    )(core.reshape(1), expert_ids, combine_weights, tokens, cotangent)


def combine_kernel(capacity, ids_ref, weights_ref, returned_ref, out_ref, back_ref, pairs_ref):
    tok_count, width = out_ref.shape
    top_count = ids_ref.shape[1]
    rows = returned_ref.shape[0]
    positions = slot_positions(ids_ref, tok_count, top_count, capacity)
    line = lax.broadcasted_iota(jnp.int32, (8, rows), 0)
    place = lax.broadcasted_iota(jnp.int32, (8, rows), 1)
    chosen = jnp.zeros((8, rows), jnp.float32)
    weighted = jnp.zeros((8, rows), jnp.float32)
    lane = lax.broadcasted_iota(jnp.int32, (1, 128), 1)
    pair_place = jnp.full((1, 128), -1, jnp.int32)
    pair_weight = jnp.ones((1, 128), jnp.float32)
    for i, position in enumerate(positions):
        n, k = divmod(i, top_count)
        here = (line == n) & (place == position)
        chosen = jnp.where(here, 1.0, chosen)
        weighted = jnp.where(here, weights_ref[n, k], weighted)
        pair_place = jnp.where(lane == i, position, pair_place)
        pair_weight = jnp.where(lane == i, weights_ref[n, k], pair_weight)
    high = weighted.astype(jnp.bfloat16)
    rest = weighted - high.astype(jnp.float32)
    middle = rest.astype(jnp.bfloat16)
    low = (rest - middle.astype(jnp.float32)).astype(jnp.bfloat16)
    terms = jnp.concatenate([high, middle, low], 0)
    plain = chosen.astype(jnp.bfloat16)
    for start in range(0, width, 512):
        values = returned_ref[:, start : start + 512]
        total = jnp.dot(terms, values, preferred_element_type=jnp.float32)
        total = total[0:8] + total[8:16] + total[16:24]
        out_ref[:, start : start + 512] = total[:tok_count].astype(jnp.bfloat16)
        values = returned_ref[:, width + start : width + start + 512]
        total = jnp.dot(plain, values, preferred_element_type=jnp.float32)
        back_ref[:, start : start + 512] = total[:tok_count].astype(jnp.bfloat16)
    extra = returned_ref[:, 2 * width : 2 * width + 128].astype(jnp.float32)
    row_values = jnp.sum(extra, 1, keepdims=True)
    match = lax.broadcasted_iota(jnp.int32, (rows, 128), 0) == pair_place
    pairs = jnp.sum(jnp.where(match, row_values, 0.0), 0, keepdims=True) / pair_weight
    for n in range(tok_count):
        pairs_ref[n : n + 1, :] = pairs[:, n * top_count : (n + 1) * top_count]


def combine_rows(expert_ids, combine_weights, returned, width, capacity):
    scalars = pl.BlockSpec(memory_space=pltpu.SMEM)
    tok_count = expert_ids.shape[0]
    half = jax.ShapeDtypeStruct((tok_count, width), jnp.bfloat16)
    return pl.pallas_call(
        functools.partial(combine_kernel, capacity),
        out_shape=(half, half, jax.ShapeDtypeStruct(expert_ids.shape, jnp.float32)),
        in_specs=[scalars, scalars, WHOLE],
        out_specs=(WHOLE, WHOLE, WHOLE),
        compiler_params=pltpu.CompilerParams(vmem_limit_bytes=8 * 1024 * 1024),
    )(expert_ids, combine_weights, returned)


def shards(sizes, tokens, expert_ids, combine_weights, cotangent, gate_weight, down_weight):
    half_width = tokens.shape[1]
    gate = gate_weight[0].T
    down = down_weight[0]
    experts = sizes[1]
    capacity = 2
    member_rows = experts * capacity

    def move(value, **shift):
        return lax.ppermute(value, AXES, shift_pairs(sizes, **shift))

    def exchange(rows):
        sent = rows.reshape(experts, capacity, rows.shape[-1])
        got = lax.all_to_all(sent, "exp", split_axis=0, concat_axis=0, tiled=True)
        return got.reshape(member_rows, rows.shape[-1])

    def add(*terms):
        return sum(t.astype(jnp.float32) for t in terms).astype(jnp.bfloat16)

    def gather(blocks, weights):
        stacked = jnp.concatenate(blocks, 0)
        across, far, gate, down = lax.optimization_barrier(
            (move(stacked, hi=1), move(stacked, row=2), *weights)
        )
        results = []
        for i, block in enumerate(blocks):
            part = slice(i * member_rows, (i + 1) * member_rows)
            pair = jnp.concatenate([block, across[part]], 0)
            results.append([pair, move(pair, row=1), move(pair, row=-1), far[part]])
        across_far = move(far, hi=1)
        for i, pieces in enumerate(results):
            part = slice(i * member_rows, (i + 1) * member_rows)
            mine = jnp.concatenate(pieces + [across_far[part]], 0)
            results[i] = (mine, move(mine, core=1))
        return results, gate, down

    def scatter_all(*halves):
        r = member_rows
        sizes_of = [r * i for i in (1, 1, 2, 2, 1, 1)]
        (kept, given), (back_kept, back_given) = halves
        first = total_blocks(kept, move(given, core=1), sizes_of)
        first_near = (move(first[2], row=-1), move(first[3], row=1))
        first_got = move(first[5], hi=1)
        back_other = move(back_given, core=1)
        second = total_blocks(back_kept, back_other, sizes_of)
        second_near = (move(second[2], row=-1), move(second[3], row=1))
        second_got = move(second[5], hi=1)
        first_far = move(add(first[4], first_got), row=2)
        second_got, _ = lax.optimization_barrier((second_got, second_near))
        second_far = move(add(second[4], second_got), row=2)
        results = []
        for total, near, straight in (
            (first, first_near, first_far),
            (second, second_near, second_far),
        ):
            across = move(add(total[1], near[0][r:], near[1][r:]), hi=1)
            results.append((total[0], *near, across, straight))
        return results

    sent, core = dispatch_rows(
        lax.axis_index("tp"), tokens, expert_ids, combine_weights, cotangent, experts, capacity
    )
    arrived = exchange(sent)
    arrived, gate, down = lax.optimization_barrier((arrived, gate, down))
    gate, down = load_weights(gate, down)
    grad_block = arrived[:, half_width:]
    (routed_rows, routed_grad), gate, down = gather(
        (arrived[:, :half_width], grad_block), (gate, down)
    )
    token_rows, token_other = routed_rows
    grad_rows, grad_other = routed_grad
    token_partial, grad_partial = expert_call(
        first_kernel, ["units", "units"], (core, token_rows, grad_rows, gate, down), 2
    )
    pre, out_kept, out_given = expert_call(
        forward_kernel, ["units", "half", "half"], (core, token_partial, token_other, gate, down), 3
    )
    back_kept, back_given = expert_call(
        backward_kernel, ["half", "half"], (core, grad_partial, grad_other, down, gate, pre), 3
    )
    out_parts, back_parts = scatter_all((out_kept, out_given), (back_kept, back_given))
    out_block = add(*[part[:member_rows] for part in out_parts])
    pair_half = jnp.sum(
        out_block.astype(jnp.float32) * grad_block.astype(jnp.float32), 1, keepdims=True
    )
    returned = exchange(
        return_payload(out_block, back_parts, pair_half, move(pair_half, core=1))
    )

    return combine_rows(expert_ids, combine_weights, returned, half_width, capacity)


def solution(mesh):
    sizes = tuple(mesh.shape[name] for name in AXES)

    def block(*args):
        return shards(sizes, *args)

    in_specs = (
        P(("ctx", "exp"), "tp"),
        P(("ctx", "exp"), None),
        P(("ctx", "exp"), None),
        P(("ctx", "exp"), "tp"),
        P("exp", None, ("ctx", "tp")),
        P("exp", ("ctx", "tp"), None),
    )
    out_specs = (P(("ctx", "exp"), "tp"), P(("ctx", "exp"), "tp"), P(("ctx", "exp"), None))
    return jax.shard_map(block, mesh=mesh, in_specs=in_specs, out_specs=out_specs, check_vma=False)
```

```python
import functools

import jax
import jax.numpy as jnp
from jax import lax
from jax.experimental import pallas as pl
from jax.experimental.pallas import tpu as pltpu
from jax.sharding import PartitionSpec as P

AXES = ("ctx", "exp", "tp")
ROW_SPLIT = 2


def shift_pairs(sizes, hi=0, row=0, core=0):
    contexts, experts, cores = sizes
    rows = contexts // ROW_SPLIT
    pairs = []
    for c in range(contexts):
        h, y = divmod(c, rows)
        target = (h + hi) % ROW_SPLIT * rows + (y + row) % rows
        for e in range(experts):
            for t in range(cores):
                pairs.append(
                    ((c * experts + e) * cores + t, (target * experts + e) * cores + (t + core) % cores)
                )
    return pairs


NT = (((1,), (1,)), ((), ()))
TILE = 512
WHOLE = pl.BlockSpec(memory_space=pltpu.VMEM)


def wide_product(rows_ref, weight_ref, half):
    width = rows_ref.shape[1]
    return lax.dot_general(
        rows_ref[...],
        weight_ref[:, half * width : (half + 1) * width],
        NT,
        preferred_element_type=jnp.float32,
    )


def deep_product(left, weight_ref, given_ref, kept_ref):
    width = kept_ref.shape[1]
    for half, out_ref in ((1, given_ref), (0, kept_ref)):
        for start in range(0, width, TILE):
            at = half * width + start
            out_ref[:, start : start + TILE] = jnp.dot(
                left, weight_ref[:, at : at + TILE], preferred_element_type=jnp.float32
            ).astype(jnp.bfloat16)


def first_kernel(rows_ref, weight_ref, partial_ref):
    partial_ref[...] = wide_product(rows_ref, weight_ref, 0)


def forward_kernel(partial_ref, other_ref, gate_ref, down_ref, pre_ref, given_ref, kept_ref):
    pre = partial_ref[...] + wide_product(other_ref, gate_ref, 1)
    pre_ref[...] = pre
    hidden = (pre / (1.0 + jnp.exp(-pre))).astype(jnp.bfloat16)
    deep_product(hidden, down_ref, given_ref, kept_ref)


def backward_kernel(
    mine_ref, other_ref, down_ref, gate_ref, pre_ref, given_ref, kept_ref
):
    grad = wide_product(mine_ref, down_ref, 0) + wide_product(other_ref, down_ref, 1)
    pre = pre_ref[...]
    sigma = 1.0 / (1.0 + jnp.exp(-pre))
    pre_grad = (grad * (sigma * (1.0 + pre * (1.0 - sigma)))).astype(jnp.bfloat16)
    deep_product(pre_grad, gate_ref, given_ref, kept_ref)


def expert_call(kernel, outs, rows, units, args, products):
    count, width = rows.shape
    shapes = {
        "units": jax.ShapeDtypeStruct((count, units), jnp.float32),
        "half": jax.ShapeDtypeStruct((count, width), jnp.bfloat16),
    }
    return pl.pallas_call(
        kernel,
        out_shape=tuple(shapes[name] for name in outs),
        in_specs=[WHOLE] * len(args),
        out_specs=tuple([WHOLE] * len(outs)),
        compiler_params=pltpu.CompilerParams(vmem_limit_bytes=24 * 1024 * 1024),
        cost_estimate=pl.CostEstimate(
            flops=2 * products * count * width * units,
            bytes_accessed=products * units * width,
            transcendentals=0,
        ),
    )(*args)


def load_kernel(core_ref, source, target, sems):
    core = core_ref[0]
    width = target.shape[1] // 2
    copies = []
    for half in range(2):
        side = core if half == 0 else 1 - core
        start = pl.multiple_of(side * width, width)
        copies.append(
            pltpu.make_async_copy(
                source.at[:, pl.ds(start, width)],
                target.at[:, pl.ds(half * width, width)],
                sems.at[half],
            )
        )
    for copy in copies:
        copy.start()
    for copy in copies:
        copy.wait()


def load_weights(core, *weights):
    return [
        pl.pallas_call(
            load_kernel,
            out_shape=jax.ShapeDtypeStruct(weight.shape, weight.dtype),
            in_specs=[pl.BlockSpec(memory_space=pltpu.SMEM), pl.BlockSpec(memory_space=pl.ANY)],
            out_specs=WHOLE,
            scratch_shapes=[pltpu.SemaphoreType.DMA((2,))],
            compiler_params=pltpu.CompilerParams(vmem_limit_bytes=44 * 1024 * 1024),
        )(core, weight)
        for weight in weights
    ]


def join_kernel(layout, *refs):
    sources, targets = refs[: len(refs) - len(layout)], refs[len(refs) - len(layout) :]
    for target, pieces in zip(targets, layout):
        at = 0
        for source, start, size in pieces:
            target[at : at + size, :] = sources[source][start : start + size, :]
            at = at + size


def join_rows(layout, *sources, after=()):
    width = sources[0].shape[1]
    return pl.pallas_call(
        functools.partial(join_kernel, layout),
        out_shape=tuple(
            jax.ShapeDtypeStruct((sum(piece[2] for piece in pieces), width), jnp.bfloat16)
            for pieces in layout
        ),
        in_specs=[WHOLE] * len(sources) + [pl.BlockSpec(memory_space=pl.ANY)] * len(after),
        out_specs=tuple([WHOLE] * len(layout)),
        compiler_params=pltpu.CompilerParams(vmem_limit_bytes=10 * 1024 * 1024),
        cost_estimate=pl.CostEstimate(flops=0, bytes_accessed=1 << 20, transcendentals=0),
    )(*sources, *after)


def total_kernel(kept_ref, got_ref, *out_refs):
    at = 0
    for out_ref in out_refs:
        size = out_ref.shape[0]
        kept = kept_ref[at : at + size, :].astype(jnp.float32)
        out_ref[...] = (kept + got_ref[at : at + size, :].astype(jnp.float32)).astype(jnp.bfloat16)
        at = at + size


def total_blocks(kept, got, sizes):
    width = kept.shape[1]
    return pl.pallas_call(
        total_kernel,
        out_shape=tuple(jax.ShapeDtypeStruct((size, width), jnp.bfloat16) for size in sizes),
        in_specs=[WHOLE, WHOLE],
        out_specs=tuple([WHOLE] * len(sizes)),
        compiler_params=pltpu.CompilerParams(vmem_limit_bytes=12 * 1024 * 1024),
        cost_estimate=pl.CostEstimate(
            flops=kept.size, bytes_accessed=1 << 20, transcendentals=0
        ),
    )(kept, got)


def payload_kernel(out_ref, own, below, above, across, straight, pair_ref, moved_ref, sent_ref):
    rows, width = out_ref.shape
    for start in range(0, width, TILE):
        cols = slice(start, start + TILE)
        sent_ref[:, cols] = out_ref[:, cols]
        total = own[:, cols].astype(jnp.float32)
        for ref in (below, above, across, straight):
            total = total + ref[:rows, cols].astype(jnp.float32)
        sent_ref[:, width + start : width + start + TILE] = total.astype(jnp.bfloat16)
    value = pair_ref[...] + moved_ref[...]
    lane = lax.broadcasted_iota(jnp.int32, (rows, 128), 1)
    extra = jnp.zeros((rows, 128), jnp.float32)
    for i in range(3):
        piece = value.astype(jnp.bfloat16).astype(jnp.float32)
        extra = jnp.where(lane == i, piece, extra)
        value = value - piece
    sent_ref[:, 2 * width :] = extra.astype(jnp.bfloat16)


def return_payload(out_block, back_parts, pair_half, moved):
    rows, width = out_block.shape
    return pl.pallas_call(
        payload_kernel,
        out_shape=jax.ShapeDtypeStruct((rows, 2 * width + 128), jnp.bfloat16),
        in_specs=[WHOLE] * 8,
        out_specs=WHOLE,
        compiler_params=pltpu.CompilerParams(vmem_limit_bytes=8 * 1024 * 1024),
    )(out_block, *back_parts, pair_half, moved)


def slot_positions(ids_ref, tok_count, top_count, capacity):
    names = [ids_ref[n, k] for n in range(tok_count) for k in range(top_count)]
    positions = []
    for i, name in enumerate(names):
        slot = jnp.int32(0)
        for other in names[:i]:
            slot = slot + jnp.where(other == name, 1, 0)
        positions.append(name * capacity + slot)
    return positions


def dispatch_kernel(
    capacity, core_ref, ids_ref, weights_ref, tokens_ref, cotangent_ref, sent_ref, core_out
):
    core_out[0] = core_ref[0]
    tok_count, width = tokens_ref.shape
    top_count = ids_ref.shape[1]
    rows = sent_ref.shape[0] * sent_ref.shape[1]
    positions = slot_positions(ids_ref, tok_count, top_count, capacity)
    place = lax.broadcasted_iota(jnp.int32, (rows, 1), 0)
    chosen, weighted = [], []
    for n in range(tok_count):
        plain = jnp.zeros((rows, 1), jnp.float32)
        scaled = jnp.zeros((rows, 1), jnp.float32)
        for k in range(top_count):
            here = place == positions[n * top_count + k]
            plain = jnp.where(here, 1.0, plain)
            scaled = jnp.where(here, weights_ref[n, k], scaled)
        chosen.append(plain)
        weighted.append(scaled)
    for source_ref, masks, base in ((tokens_ref, chosen, 0), (cotangent_ref, weighted, width)):
        for start in range(0, width, 512):
            values = source_ref[:, start : start + 512].astype(jnp.float32)
            total = masks[0] * values[0:1]
            for n in range(1, tok_count):
                total = total + masks[n] * values[n : n + 1]
            shaped = total.astype(jnp.bfloat16).reshape(rows // capacity, capacity, 512)
            sent_ref[:, :, base + start : base + start + 512] = shaped


def dispatch_rows(core, tokens, expert_ids, combine_weights, cotangent, experts, capacity):
    scalars = pl.BlockSpec(memory_space=pltpu.SMEM)
    return pl.pallas_call(
        functools.partial(dispatch_kernel, capacity),
        out_shape=(
            jax.ShapeDtypeStruct((experts, capacity, 2 * tokens.shape[1]), jnp.bfloat16),
            jax.ShapeDtypeStruct((1,), jnp.int32),
        ),
        in_specs=[scalars, scalars, scalars, WHOLE, WHOLE],
        out_specs=(WHOLE, scalars),
        compiler_params=pltpu.CompilerParams(vmem_limit_bytes=58 * 1024 * 1024),
    )(core.reshape(1), expert_ids, combine_weights, tokens, cotangent)


def combine_kernel(capacity, ids_ref, weights_ref, returned_ref, out_ref, back_ref, pairs_ref):
    tok_count, width = out_ref.shape
    top_count = ids_ref.shape[1]
    rows = returned_ref.shape[0]
    positions = slot_positions(ids_ref, tok_count, top_count, capacity)
    line = lax.broadcasted_iota(jnp.int32, (8, rows), 0)
    place = lax.broadcasted_iota(jnp.int32, (8, rows), 1)
    chosen = jnp.zeros((8, rows), jnp.float32)
    weighted = jnp.zeros((8, rows), jnp.float32)
    lane = lax.broadcasted_iota(jnp.int32, (1, 128), 1)
    pair_place = jnp.full((1, 128), -1, jnp.int32)
    pair_weight = jnp.ones((1, 128), jnp.float32)
    for i, position in enumerate(positions):
        n, k = divmod(i, top_count)
        here = (line == n) & (place == position)
        chosen = jnp.where(here, 1.0, chosen)
        weighted = jnp.where(here, weights_ref[n, k], weighted)
        pair_place = jnp.where(lane == i, position, pair_place)
        pair_weight = jnp.where(lane == i, weights_ref[n, k], pair_weight)
    high = weighted.astype(jnp.bfloat16)
    rest = weighted - high.astype(jnp.float32)
    middle = rest.astype(jnp.bfloat16)
    low = (rest - middle.astype(jnp.float32)).astype(jnp.bfloat16)
    terms = jnp.concatenate([high, middle, low], 0)
    plain = chosen.astype(jnp.bfloat16)
    total = jnp.dot(terms, returned_ref[:, :width], preferred_element_type=jnp.float32)
    total = total[0:8] + total[8:16] + total[16:24]
    out_ref[...] = total[:tok_count].astype(jnp.bfloat16)
    total = jnp.dot(
        plain, returned_ref[:, width : 2 * width], preferred_element_type=jnp.float32
    )
    back_ref[...] = total[:tok_count].astype(jnp.bfloat16)
    extra = returned_ref[:, 2 * width : 2 * width + 128].astype(jnp.float32)
    row_values = jnp.sum(extra, 1, keepdims=True)
    match = lax.broadcasted_iota(jnp.int32, (rows, 128), 0) == pair_place
    pairs = jnp.sum(jnp.where(match, row_values, 0.0), 0, keepdims=True) / pair_weight
    for n in range(tok_count):
        pairs_ref[n : n + 1, :] = pairs[:, n * top_count : (n + 1) * top_count]


def combine_rows(expert_ids, combine_weights, returned, width, capacity):
    scalars = pl.BlockSpec(memory_space=pltpu.SMEM)
    tok_count = expert_ids.shape[0]
    half = jax.ShapeDtypeStruct((tok_count, width), jnp.bfloat16)
    return pl.pallas_call(
        functools.partial(combine_kernel, capacity),
        out_shape=(half, half, jax.ShapeDtypeStruct(expert_ids.shape, jnp.float32)),
        in_specs=[scalars, scalars, WHOLE],
        out_specs=(WHOLE, WHOLE, WHOLE),
        compiler_params=pltpu.CompilerParams(vmem_limit_bytes=8 * 1024 * 1024),
    )(expert_ids, combine_weights, returned)


def shards(sizes, tokens, expert_ids, combine_weights, cotangent, gate_weight, down_weight):
    half_width = tokens.shape[1]
    gate = gate_weight[0].T
    down = down_weight[0]
    experts = sizes[1]
    capacity = 2
    member_rows = experts * capacity

    def move(value, **shift):
        return lax.ppermute(value, AXES, shift_pairs(sizes, **shift))

    def exchange(rows):
        sent = rows.reshape(experts, capacity, rows.shape[-1])
        got = lax.all_to_all(sent, "exp", split_axis=0, concat_axis=0, tiled=True)
        return got.reshape(member_rows, rows.shape[-1])

    def add(*terms):
        return sum(t.astype(jnp.float32) for t in terms).astype(jnp.bfloat16)

    def gather(blocks, weights):
        stacked = jnp.concatenate(blocks, 0)
        across, far, gate, down = lax.optimization_barrier(
            (move(stacked, hi=1), move(stacked, row=2), *weights)
        )
        results = []
        for i, block in enumerate(blocks):
            part = slice(i * member_rows, (i + 1) * member_rows)
            pair = jnp.concatenate([block, across[part]], 0)
            results.append([pair, move(pair, row=1), move(pair, row=-1), far[part]])
        across_far = move(far, hi=1)
        for i, pieces in enumerate(results):
            part = slice(i * member_rows, (i + 1) * member_rows)
            mine = jnp.concatenate(pieces + [across_far[part]], 0)
            results[i] = (mine, move(mine, core=1))
        return results, gate, down

    def scatter_all(*halves):
        r = member_rows
        sizes_of = [r * i for i in (1, 1, 2, 2, 1, 1)]
        (kept, given), (back_kept, back_given) = halves
        first = total_blocks(kept, move(given, core=1), sizes_of)
        first_near = (move(first[2], row=-1), move(first[3], row=1))
        first_got = move(first[5], hi=1)
        back_other = move(back_given, core=1)
        second = total_blocks(back_kept, back_other, sizes_of)
        second_near = (move(second[2], row=-1), move(second[3], row=1))
        second_got = move(second[5], hi=1)
        first_far = move(add(first[4], first_got), row=2)
        second_got, _ = lax.optimization_barrier((second_got, second_near))
        second_far = move(add(second[4], second_got), row=2)
        results = []
        for total, near, straight in (
            (first, first_near, first_far),
            (second, second_near, second_far),
        ):
            across = move(add(total[1], near[0][r:], near[1][r:]), hi=1)
            results.append((total[0], *near, across, straight))
        return results

    sent, core = dispatch_rows(
        lax.axis_index("tp"), tokens, expert_ids, combine_weights, cotangent, experts, capacity
    )
    arrived = exchange(sent)
    r = member_rows
    grad_block = arrived[:, half_width:]
    stacked = jnp.concatenate([arrived[:, :half_width], grad_block], 0)
    stacked, gate, down = lax.optimization_barrier((stacked, gate, down))
    across, far = move(stacked, hi=1), move(stacked, row=2)
    across, far, gate, down = lax.optimization_barrier((across, far, *load_weights(core, gate, down)))
    pairs = join_rows([[(0, i, r), (1, i, r)] for i in (0, r)], stacked, across)
    token_pair, grad_pair = pairs
    below, above = zip(*[(move(pair, row=1), move(pair, row=-1)) for pair in pairs])
    across_far = move(far, hi=1)

    def join_mine(i, after=()):
        layout = [(0, 0, 2 * r), (1, 0, 2 * r), (2, 0, 2 * r), (3, i * r, r), (4, i * r, r)]
        return join_rows(
            [layout], pairs[i], below[i], above[i], far, across_far, after=after
        )[0]

    token_rows = join_mine(0)
    token_other = move(token_rows, core=1)
    units = down.shape[0]
    (token_partial,) = expert_call(
        first_kernel, ["units"], token_rows, units, (token_rows, gate), 1
    )
    grad_rows = join_mine(1, (token_partial,))
    grad_other = move(grad_rows, core=1)
    pre, out_given, out_kept = expert_call(
        forward_kernel,
        ["units", "half", "half"],
        token_rows,
        units,
        (token_partial, token_other, gate, down),
        3,
    )
    back_given, back_kept = expert_call(
        backward_kernel, ["half", "half"], grad_rows, units, (grad_rows, grad_other, down, gate, pre), 4
    )
    out_parts, back_parts = scatter_all((out_kept, out_given), (back_kept, back_given))
    out_block = add(*[part[:member_rows] for part in out_parts])
    pair_half = jnp.sum(
        out_block.astype(jnp.float32) * grad_block.astype(jnp.float32), 1, keepdims=True
    )
    returned = exchange(
        return_payload(out_block, back_parts, pair_half, move(pair_half, core=1))
    )

    return combine_rows(expert_ids, combine_weights, returned, half_width, capacity)


def solution(mesh):
    sizes = tuple(mesh.shape[name] for name in AXES)

    def block(*args):
        return shards(sizes, *args)

    in_specs = (
        P(("ctx", "exp"), "tp"),
        P(("ctx", "exp"), None),
        P(("ctx", "exp"), None),
        P(("ctx", "exp"), "tp"),
        P("exp", None, ("ctx", "tp")),
        P("exp", ("ctx", "tp"), None),
    )
    out_specs = (P(("ctx", "exp"), "tp"), P(("ctx", "exp"), "tp"), P(("ctx", "exp"), None))
    return jax.shard_map(block, mesh=mesh, in_specs=in_specs, out_specs=out_specs, check_vma=False)
```

```python
import functools

import jax
import jax.numpy as jnp
from jax import lax
from jax.experimental import pallas as pl
from jax.experimental.pallas import tpu as pltpu
from jax.sharding import PartitionSpec as P

AXES = ("ctx", "exp", "tp")
ROW_SPLIT = 2


def shift_pairs(sizes, hi=0, row=0, core=0):
    contexts, experts, cores = sizes
    rows = contexts // ROW_SPLIT
    pairs = []
    for c in range(contexts):
        h, y = divmod(c, rows)
        target = (h + hi) % ROW_SPLIT * rows + (y + row) % rows
        for e in range(experts):
            for t in range(cores):
                pairs.append(
                    ((c * experts + e) * cores + t, (target * experts + e) * cores + (t + core) % cores)
                )
    return pairs


NT = (((1,), (1,)), ((), ()))
TILE = 512
WHOLE = pl.BlockSpec(memory_space=pltpu.VMEM)


def wide_product(rows_ref, weight_ref, half):
    width = rows_ref.shape[1]
    return lax.dot_general(
        rows_ref[...],
        weight_ref[:, half * width : (half + 1) * width],
        NT,
        preferred_element_type=jnp.float32,
    )


def deep_product(left, weight_ref, given_ref, kept_ref):
    width = kept_ref.shape[1]
    for half, out_ref in ((1, given_ref), (0, kept_ref)):
        for start in range(0, width, TILE):
            at = half * width + start
            out_ref[:, start : start + TILE] = jnp.dot(
                left, weight_ref[:, at : at + TILE], preferred_element_type=jnp.float32
            ).astype(jnp.bfloat16)


def first_kernel(rows_ref, weight_ref, partial_ref):
    partial_ref[...] = wide_product(rows_ref, weight_ref, 0)


def forward_kernel(partial_ref, other_ref, gate_ref, down_ref, pre_ref, given_ref, kept_ref):
    pre = partial_ref[...] + wide_product(other_ref, gate_ref, 1)
    pre_ref[...] = pre
    hidden = (pre / (1.0 + jnp.exp(-pre))).astype(jnp.bfloat16)
    deep_product(hidden, down_ref, given_ref, kept_ref)


def backward_kernel(
    mine_ref, other_ref, down_ref, gate_ref, pre_ref, given_ref, kept_ref
):
    grad = wide_product(mine_ref, down_ref, 0) + wide_product(other_ref, down_ref, 1)
    pre = pre_ref[...]
    sigma = 1.0 / (1.0 + jnp.exp(-pre))
    pre_grad = (grad * (sigma * (1.0 + pre * (1.0 - sigma)))).astype(jnp.bfloat16)
    deep_product(pre_grad, gate_ref, given_ref, kept_ref)


def expert_call(kernel, outs, rows, units, args, products):
    count, width = rows.shape
    shapes = {
        "units": jax.ShapeDtypeStruct((count, units), jnp.float32),
        "half": jax.ShapeDtypeStruct((count, width), jnp.bfloat16),
    }
    return pl.pallas_call(
        kernel,
        out_shape=tuple(shapes[name] for name in outs),
        in_specs=[WHOLE] * len(args),
        out_specs=tuple([WHOLE] * len(outs)),
        compiler_params=pltpu.CompilerParams(vmem_limit_bytes=24 * 1024 * 1024),
        cost_estimate=pl.CostEstimate(
            flops=2 * products * count * width * units,
            bytes_accessed=products * units * width,
            transcendentals=0,
        ),
    )(*args)


def load_kernel(core_ref, source, target, sems):
    core = core_ref[0]
    width = target.shape[1] // 2
    copies = []
    for half in range(2):
        side = core if half == 0 else 1 - core
        start = pl.multiple_of(side * width, width)
        copies.append(
            pltpu.make_async_copy(
                source.at[:, pl.ds(start, width)],
                target.at[:, pl.ds(half * width, width)],
                sems.at[half],
            )
        )
    for copy in copies:
        copy.start()
    for copy in copies:
        copy.wait()


def load_weights(core, *weights):
    return [
        pl.pallas_call(
            load_kernel,
            out_shape=jax.ShapeDtypeStruct(weight.shape, weight.dtype),
            in_specs=[pl.BlockSpec(memory_space=pltpu.SMEM), pl.BlockSpec(memory_space=pl.ANY)],
            out_specs=WHOLE,
            scratch_shapes=[pltpu.SemaphoreType.DMA((2,))],
            compiler_params=pltpu.CompilerParams(vmem_limit_bytes=44 * 1024 * 1024),
        )(core, weight)
        for weight in weights
    ]


def join_kernel(layout, *refs):
    sources, targets = refs[: len(refs) - len(layout)], refs[len(refs) - len(layout) :]
    for target, pieces in zip(targets, layout):
        at = 0
        for source, start, size in pieces:
            target[at : at + size, :] = sources[source][start : start + size, :]
            at = at + size


def join_rows(layout, *sources, after=()):
    width = sources[0].shape[1]
    return pl.pallas_call(
        functools.partial(join_kernel, layout),
        out_shape=tuple(
            jax.ShapeDtypeStruct((sum(piece[2] for piece in pieces), width), jnp.bfloat16)
            for pieces in layout
        ),
        in_specs=[WHOLE] * len(sources) + [pl.BlockSpec(memory_space=pl.ANY)] * len(after),
        out_specs=tuple([WHOLE] * len(layout)),
        compiler_params=pltpu.CompilerParams(vmem_limit_bytes=10 * 1024 * 1024),
        cost_estimate=pl.CostEstimate(flops=0, bytes_accessed=1 << 20, transcendentals=0),
    )(*sources, *after)


def total_kernel(kept_ref, got_ref, *out_refs):
    at = 0
    for out_ref in out_refs:
        size = out_ref.shape[0]
        kept = kept_ref[at : at + size, :].astype(jnp.float32)
        out_ref[...] = (kept + got_ref[at : at + size, :].astype(jnp.float32)).astype(jnp.bfloat16)
        at = at + size


def total_blocks(kept, got, sizes):
    width = kept.shape[1]
    return pl.pallas_call(
        total_kernel,
        out_shape=tuple(jax.ShapeDtypeStruct((size, width), jnp.bfloat16) for size in sizes),
        in_specs=[WHOLE, WHOLE],
        out_specs=tuple([WHOLE] * len(sizes)),
        compiler_params=pltpu.CompilerParams(vmem_limit_bytes=12 * 1024 * 1024),
        cost_estimate=pl.CostEstimate(
            flops=kept.size, bytes_accessed=1 << 20, transcendentals=0
        ),
    )(kept, got)


def payload_kernel(out_ref, own, below, above, across, straight, pair_ref, moved_ref, sent_ref):
    rows, width = out_ref.shape
    for start in range(0, width, TILE):
        cols = slice(start, start + TILE)
        sent_ref[:, cols] = out_ref[:, cols]
        total = own[:, cols].astype(jnp.float32)
        for ref in (below, above, across, straight):
            total = total + ref[:rows, cols].astype(jnp.float32)
        sent_ref[:, width + start : width + start + TILE] = total.astype(jnp.bfloat16)
    value = pair_ref[...] + moved_ref[...]
    lane = lax.broadcasted_iota(jnp.int32, (rows, 128), 1)
    extra = jnp.zeros((rows, 128), jnp.float32)
    for i in range(3):
        piece = value.astype(jnp.bfloat16).astype(jnp.float32)
        extra = jnp.where(lane == i, piece, extra)
        value = value - piece
    sent_ref[:, 2 * width :] = extra.astype(jnp.bfloat16)


def return_payload(out_block, back_parts, pair_half, moved):
    rows, width = out_block.shape
    return pl.pallas_call(
        payload_kernel,
        out_shape=jax.ShapeDtypeStruct((rows, 2 * width + 128), jnp.bfloat16),
        in_specs=[WHOLE] * 8,
        out_specs=WHOLE,
        compiler_params=pltpu.CompilerParams(vmem_limit_bytes=8 * 1024 * 1024),
    )(out_block, *back_parts, pair_half, moved)


def slot_positions(ids_ref, tok_count, top_count, capacity):
    names = [ids_ref[n, k] for n in range(tok_count) for k in range(top_count)]
    positions = []
    for i, name in enumerate(names):
        slot = jnp.int32(0)
        for other in names[:i]:
            slot = slot + jnp.where(other == name, 1, 0)
        positions.append(name * capacity + slot)
    return positions


def dispatch_kernel(
    capacity, core_ref, ids_ref, weights_ref, tokens_ref, cotangent_ref, sent_ref, core_out
):
    core_out[0] = core_ref[0]
    tok_count, width = tokens_ref.shape
    top_count = ids_ref.shape[1]
    rows = sent_ref.shape[0] * sent_ref.shape[1]
    positions = slot_positions(ids_ref, tok_count, top_count, capacity)
    place = lax.broadcasted_iota(jnp.int32, (rows, 1), 0)
    chosen, weighted = [], []
    for n in range(tok_count):
        plain = jnp.zeros((rows, 1), jnp.float32)
        scaled = jnp.zeros((rows, 1), jnp.float32)
        for k in range(top_count):
            here = place == positions[n * top_count + k]
            plain = jnp.where(here, 1.0, plain)
            scaled = jnp.where(here, weights_ref[n, k], scaled)
        chosen.append(plain)
        weighted.append(scaled)
    for source_ref, masks, base in ((tokens_ref, chosen, 0), (cotangent_ref, weighted, width)):
        for start in range(0, width, 512):
            values = source_ref[:, start : start + 512].astype(jnp.float32)
            total = masks[0] * values[0:1]
            for n in range(1, tok_count):
                total = total + masks[n] * values[n : n + 1]
            shaped = total.astype(jnp.bfloat16).reshape(rows // capacity, capacity, 512)
            sent_ref[:, :, base + start : base + start + 512] = shaped


def dispatch_rows(core, tokens, expert_ids, combine_weights, cotangent, experts, capacity):
    scalars = pl.BlockSpec(memory_space=pltpu.SMEM)
    return pl.pallas_call(
        functools.partial(dispatch_kernel, capacity),
        out_shape=(
            jax.ShapeDtypeStruct((experts, capacity, 2 * tokens.shape[1]), jnp.bfloat16),
            jax.ShapeDtypeStruct((1,), jnp.int32),
        ),
        in_specs=[scalars, scalars, scalars, WHOLE, WHOLE],
        out_specs=(WHOLE, scalars),
        compiler_params=pltpu.CompilerParams(vmem_limit_bytes=58 * 1024 * 1024),
    )(core.reshape(1), expert_ids, combine_weights, tokens, cotangent)


def combine_kernel(capacity, ids_ref, weights_ref, returned_ref, out_ref, back_ref, pairs_ref):
    tok_count, width = out_ref.shape
    top_count = ids_ref.shape[1]
    rows = returned_ref.shape[0]
    positions = slot_positions(ids_ref, tok_count, top_count, capacity)
    line = lax.broadcasted_iota(jnp.int32, (8, rows), 0)
    place = lax.broadcasted_iota(jnp.int32, (8, rows), 1)
    chosen = jnp.zeros((8, rows), jnp.float32)
    weighted = jnp.zeros((8, rows), jnp.float32)
    lane = lax.broadcasted_iota(jnp.int32, (1, 128), 1)
    pair_place = jnp.full((1, 128), -1, jnp.int32)
    pair_weight = jnp.ones((1, 128), jnp.float32)
    for i, position in enumerate(positions):
        n, k = divmod(i, top_count)
        here = (line == n) & (place == position)
        chosen = jnp.where(here, 1.0, chosen)
        weighted = jnp.where(here, weights_ref[n, k], weighted)
        pair_place = jnp.where(lane == i, position, pair_place)
        pair_weight = jnp.where(lane == i, weights_ref[n, k], pair_weight)
    high = weighted.astype(jnp.bfloat16)
    rest = weighted - high.astype(jnp.float32)
    middle = rest.astype(jnp.bfloat16)
    low = (rest - middle.astype(jnp.float32)).astype(jnp.bfloat16)
    terms = jnp.concatenate([high, middle, low], 0)
    plain = chosen.astype(jnp.bfloat16)
    total = jnp.dot(terms, returned_ref[:, :width], preferred_element_type=jnp.float32)
    total = total[0:8] + total[8:16] + total[16:24]
    out_ref[...] = total[:tok_count].astype(jnp.bfloat16)
    total = jnp.dot(
        plain, returned_ref[:, width : 2 * width], preferred_element_type=jnp.float32
    )
    back_ref[...] = total[:tok_count].astype(jnp.bfloat16)
    extra = returned_ref[:, 2 * width : 2 * width + 128].astype(jnp.float32)
    row_values = jnp.sum(extra, 1, keepdims=True)
    match = lax.broadcasted_iota(jnp.int32, (rows, 128), 0) == pair_place
    pairs = jnp.sum(jnp.where(match, row_values, 0.0), 0, keepdims=True) / pair_weight
    for n in range(tok_count):
        pairs_ref[n : n + 1, :] = pairs[:, n * top_count : (n + 1) * top_count]


def combine_rows(expert_ids, combine_weights, returned, width, capacity):
    scalars = pl.BlockSpec(memory_space=pltpu.SMEM)
    tok_count = expert_ids.shape[0]
    half = jax.ShapeDtypeStruct((tok_count, width), jnp.bfloat16)
    return pl.pallas_call(
        functools.partial(combine_kernel, capacity),
        out_shape=(half, half, jax.ShapeDtypeStruct(expert_ids.shape, jnp.float32)),
        in_specs=[scalars, scalars, WHOLE],
        out_specs=(WHOLE, WHOLE, WHOLE),
        compiler_params=pltpu.CompilerParams(vmem_limit_bytes=8 * 1024 * 1024),
    )(expert_ids, combine_weights, returned)


def shards(sizes, tokens, expert_ids, combine_weights, cotangent, gate_weight, down_weight):
    half_width = tokens.shape[1]
    gate = gate_weight[0].T
    down = down_weight[0]
    experts = sizes[1]
    capacity = 2
    member_rows = experts * capacity

    def move(value, **shift):
        return lax.ppermute(value, AXES, shift_pairs(sizes, **shift))

    def exchange(rows):
        sent = rows.reshape(experts, capacity, rows.shape[-1])
        got = lax.all_to_all(sent, "exp", split_axis=0, concat_axis=0, tiled=True)
        return got.reshape(member_rows, rows.shape[-1])

    def add(*terms):
        return sum(t.astype(jnp.float32) for t in terms).astype(jnp.bfloat16)

    def gather(blocks, weights):
        stacked = jnp.concatenate(blocks, 0)
        across, far, gate, down = lax.optimization_barrier(
            (move(stacked, hi=1), move(stacked, row=2), *weights)
        )
        results = []
        for i, block in enumerate(blocks):
            part = slice(i * member_rows, (i + 1) * member_rows)
            pair = jnp.concatenate([block, across[part]], 0)
            results.append([pair, move(pair, row=1), move(pair, row=-1), far[part]])
        across_far = move(far, hi=1)
        for i, pieces in enumerate(results):
            part = slice(i * member_rows, (i + 1) * member_rows)
            mine = jnp.concatenate(pieces + [across_far[part]], 0)
            results[i] = (mine, move(mine, core=1))
        return results, gate, down

    def scatter_all(*halves):
        r = member_rows
        sizes_of = [r * i for i in (1, 1, 2, 2, 1, 1)]
        (kept, given), (back_kept, back_given) = halves
        first = total_blocks(kept, move(given, core=1), sizes_of)
        first_near = (move(first[2], row=-1), move(first[3], row=1))
        first_got = move(first[5], hi=1)
        back_other = move(back_given, core=1)
        second = total_blocks(back_kept, back_other, sizes_of)
        second_near = (move(second[2], row=-1), move(second[3], row=1))
        second_got = move(second[5], hi=1)
        first_far = move(add(first[4], first_got), row=2)
        first_across = move(add(first[1], first_near[0][r:], first_near[1][r:]), hi=1)
        second_got, _ = lax.optimization_barrier((second_got, first_across))
        second_far = move(add(second[4], second_got), row=2)
        second_across = move(add(second[1], second_near[0][r:], second_near[1][r:]), hi=1)
        return [
            (first[0], *first_near, first_across, first_far),
            (second[0], *second_near, second_across, second_far),
        ]

    sent, core = dispatch_rows(
        lax.axis_index("tp"), tokens, expert_ids, combine_weights, cotangent, experts, capacity
    )
    arrived = exchange(sent)
    r = member_rows
    grad_block = arrived[:, half_width:]
    stacked = jnp.concatenate([arrived[:, :half_width], grad_block], 0)
    stacked, gate, down = lax.optimization_barrier((stacked, gate, down))
    across, far = move(stacked, hi=1), move(stacked, row=2)
    across, far, gate, down = lax.optimization_barrier((across, far, *load_weights(core, gate, down)))
    pairs = join_rows([[(0, i, r), (1, i, r)] for i in (0, r)], stacked, across)
    token_pair, grad_pair = pairs
    above, below = zip(*[(move(pair, row=-1), move(pair, row=1)) for pair in pairs])
    across_far = move(far, hi=1)

    def join_mine(i, after=()):
        layout = [(0, 0, 2 * r), (1, 0, 2 * r), (2, 0, 2 * r), (3, i * r, r), (4, i * r, r)]
        return join_rows(
            [layout], pairs[i], below[i], above[i], far, across_far, after=after
        )[0]

    token_rows = join_mine(0)
    token_other = move(token_rows, core=1)
    units = down.shape[0]
    (token_partial,) = expert_call(
        first_kernel, ["units"], token_rows, units, (token_rows, gate), 1
    )
    grad_rows = join_mine(1, (token_partial,))
    grad_other = move(grad_rows, core=1)
    pre, out_given, out_kept = expert_call(
        forward_kernel,
        ["units", "half", "half"],
        token_rows,
        units,
        (token_partial, token_other, gate, down),
        3,
    )
    back_given, back_kept = expert_call(
        backward_kernel, ["half", "half"], grad_rows, units, (grad_rows, grad_other, down, gate, pre), 4
    )
    out_parts, back_parts = scatter_all((out_kept, out_given), (back_kept, back_given))
    out_block = add(*[part[:member_rows] for part in out_parts])
    pair_half = jnp.sum(
        out_block.astype(jnp.float32) * grad_block.astype(jnp.float32), 1, keepdims=True
    )
    returned = exchange(
        return_payload(out_block, back_parts, pair_half, move(pair_half, core=1))
    )

    return combine_rows(expert_ids, combine_weights, returned, half_width, capacity)


def solution(mesh):
    sizes = tuple(mesh.shape[name] for name in AXES)

    def block(*args):
        return shards(sizes, *args)

    in_specs = (
        P(("ctx", "exp"), "tp"),
        P(("ctx", "exp"), None),
        P(("ctx", "exp"), None),
        P(("ctx", "exp"), "tp"),
        P("exp", None, ("ctx", "tp")),
        P("exp", ("ctx", "tp"), None),
    )
    out_specs = (P(("ctx", "exp"), "tp"), P(("ctx", "exp"), "tp"), P(("ctx", "exp"), None))
    return jax.shard_map(block, mesh=mesh, in_specs=in_specs, out_specs=out_specs, check_vma=False)
```
